32 devices in a mesh: tensor: 2 (over core), row: 4 (over y, x), col: 4 (over z).
Axes of the slice: x: 2, y: 2, z: 4, core: 2. Of those that a mesh axis runs over, the one named last changes fastest.
Arguments:
- integral_tiles: bfloat16 [256, 8, 4096], P(('tensor', 'row', 'col')), may hold values from -6 to 6
- tile_index: int32 [256, 3], P(('tensor', 'row', 'col')), may hold values from 0 to 63, as said below
- virtual_coeff: bfloat16 [4096, 2048], P('col'), may hold values from -0.125 to 0.125
- occupied_coeff: bfloat16 [512, 512], P('row'), may hold values from -0.25 to 0.25
Outputs:
- pair_tensor: bfloat16 [2048, 32, 512], P(('row', 'col'), 'tensor')
The draws below stay inside these ranges and needn't reach their ends.
Inputs may be any that keep to these rules, and one draw needn't show every extreme that they name: `tile_index`: the tiles of the device at index (t, r, c) of tensor, row, col all have their nu block in c * 16 .. (c + 1) * 16 - 1, their auxiliary block below 4 and their mu block below 8. A tile's owner is (tensor index a // 2, row index m // 2) in the same col. Each device holds at most 2 tiles for any one owner; in every draw some owner gets exactly 2 tiles from every device of its col. Tiles with equal indices may occur and add up.
All inputs are finite; a program needn't handle non-finite values.
Results may differ from the reference program's by a relative error of at most 0.025.
Values may be sent and summed in bfloat16 or wider, within the bound.
A program may use at most 128 MiB of HBM per device.

```python
import jax
import jax.numpy as jnp
from jax import lax

TB = 64
PB = 8
AB = 2
MB = 2
NBC = 16
CAP = 2
NV = 2048
NOCC = 512
K_DEV = 8
NMU = 8
NNU = 64
TILES = 256
N_TENSOR = 2
N_ROW = 4
N_COL = 4


def draw_tile_index(key, part):
    owners = N_TENSOR * N_ROW
    sources = N_TENSOR * N_ROW * N_COL
    hot_count = owners // 4
    order = jax.random.permutation(jax.random.fold_in(key, 11), owners)
    hot_slots = jnp.repeat(order[:hot_count], CAP)
    cold_slots = jnp.repeat(order[hot_count:], CAP)
    half_held = K_DEV // 2

    def one_device(device_key):
        picked = jax.random.permutation(jax.random.fold_in(device_key, 1), cold_slots.shape[0])[:half_held]
        target = jnp.concatenate([hot_slots, cold_slots[picked]])
        target = target[jax.random.permutation(jax.random.fold_in(device_key, 2), K_DEV)]
        aux_local = jax.random.randint(jax.random.fold_in(device_key, 3), (K_DEV,), 0, AB)
        mu_local = jax.random.randint(jax.random.fold_in(device_key, 4), (K_DEV,), 0, MB)
        nu_local = jax.random.randint(jax.random.fold_in(device_key, 5), (K_DEV,), 0, NBC)
        nu_local = nu_local.at[0].set(NBC - 1).at[1].set(0)
        return (target, aux_local, mu_local, nu_local)
    device_keys = jax.random.split(jax.random.fold_in(key, 13), sources)
    target, aux_local, mu_local, nu_local = jax.vmap(one_device)(device_keys)
    column = (jnp.arange(sources, dtype=jnp.int32) % N_COL)[:, None]
    aux_block = target // N_ROW * AB + aux_local
    mu_block = target % N_ROW * MB + mu_local
    nu_block = column * NBC + nu_local
    stacked = jnp.stack([aux_block, mu_block, nu_block], axis=-1)
    return stacked.reshape(sources * K_DEV, 3).astype(jnp.int32)


def spiked(array, stream_key, source, target, parts, factor):
    owner, partner = [(jnp.arange(array.shape[position]) // (array.shape[position] // parts)).reshape([-1 if axis == position else 1 for axis in range(array.ndim)]) for position in (source, target)]
    chosen = jax.random.permutation(stream_key, parts)[partner]
    strong = (owner == chosen) | (owner == (partner + parts // 2) % parts)
    return jnp.where(strong, factor * array, array)


def steps_of(own_key, extent, shards, smallest, largest):
    loudness, own = 1.0, jax.random.fold_in(own_key, 6)
    for axis_at, blocks in shards:
        heights = jnp.exp(jax.random.uniform(jax.random.fold_in(own, axis_at), (blocks,), jnp.float32, smallest / len(shards), largest / len(shards)))
        loudness = loudness * jnp.repeat(heights, extent[axis_at] // blocks).reshape([-1 if axis == axis_at else 1 for axis in range(len(extent))])
    return loudness


def normal_values(stream_key, dims, deviation, bound, cuts=(), kind=jnp.bfloat16):
    array = jax.random.normal(stream_key, dims, jnp.float32) * deviation
    if len(cuts) > 0:
        array = steps_of(stream_key, dims, cuts, -0.22, 0.18) * array
    return jnp.clip(array, min=-bound, max=bound).astype(kind)


def bell_draw_with(key, dims, deviation, most, cuts, heavy, held_as=jnp.bfloat16):
    values = deviation * jax.random.normal(key, dims, jnp.float32)
    if cuts:
        values = values * steps_of(key, dims, cuts, -0.22, 0.18)
    return jnp.clip(spiked(values, jax.random.fold_in(key, 3), *heavy), -most, most).astype(held_as)


def setup_inputs(seed: int = 0) -> dict:
    keys = jax.random.split(jax.random.key(seed), 5)
    integral_tiles = normal_values(keys[0], (TILES, PB, TB * TB), 1.0, 6.0, ((0, 32),))
    tile_index = draw_tile_index(jax.random.fold_in(keys[4], 71), 0)
    virtual_coeff = bell_draw_with(keys[2], (NNU * TB, NV), (NNU * TB) ** -0.5, 0.125, ((0, 4),), (0, 1, 4, 2.0))
    occupied_coeff = normal_values(keys[3], (NMU * TB, NOCC), (NMU * TB) ** -0.5, 0.25, ((0, 4),))
    return dict(integral_tiles=integral_tiles, tile_index=tile_index, virtual_coeff=virtual_coeff, occupied_coeff=occupied_coeff)


def reference(integral_tiles, tile_index, virtual_coeff, occupied_coeff):
    groups = N_TENSOR * N_ROW
    held = integral_tiles.shape[0] // (groups * N_COL)
    tile_len = PB * TB * TB
    by_column = jnp.moveaxis(integral_tiles.reshape(groups, N_COL, held, tile_len), 1, 0).reshape(N_COL, groups * held, tile_len)
    index_cols = jnp.moveaxis(tile_index.reshape(groups, N_COL, held, 3), 1, 0).reshape(N_COL, groups * held, 3)
    coeff_cols = virtual_coeff.reshape(N_COL, NBC, TB, NV)
    aux_blocks = N_TENSOR * AB
    mu_blocks = N_ROW * MB
    segments = aux_blocks * mu_blocks * NBC

    def add_column(total, pieces):
        tiles, index, coeff, column = pieces
        segment = (index[:, 0] * mu_blocks + index[:, 1]) * NBC + index[:, 2] - column * NBC
        dense = jax.ops.segment_sum(tiles.astype(jnp.float32), segment.astype(jnp.int32), num_segments=segments)
        dense = dense.astype(jnp.bfloat16).reshape(aux_blocks, mu_blocks, NBC, PB, TB, TB)
        part = jnp.einsum("knv,amkpun->vampu", coeff.astype(jnp.float32), dense.astype(jnp.float32))
        part = lax.optimization_barrier(part.astype(jnp.bfloat16))
        return total + part.astype(jnp.float32), None

    start_total = jnp.zeros((NV, aux_blocks, mu_blocks, PB, TB), jnp.float32)
    columns = jnp.arange(N_COL, dtype=jnp.int32)
    total, unused = lax.scan(add_column, start_total, (by_column, index_cols, coeff_cols, columns))
    half = total.astype(jnp.bfloat16)
    occupied = occupied_coeff.reshape(mu_blocks, TB, NOCC).astype(jnp.float32)
    result = jnp.einsum("vampu,muo->vapo", half.astype(jnp.float32), occupied)
    return result.reshape(NV, aux_blocks * PB, NOCC).astype(jnp.bfloat16)
```

```python
import jax
import jax.numpy as jnp
from jax import lax
from jax.experimental import pallas as pl
from jax.experimental.pallas import tpu as pltpu
from jax.sharding import PartitionSpec as P

TB = 64
PB = 8
AB = 2
MB = 2
NBC = 16
CAP = 2
NV = 2048
NOCC = 512


def shards(integral_tiles, tile_index, virtual_coeff, occupied_coeff):
    tensor_at = lax.axis_index("tensor")
    row_at = lax.axis_index("row")
    col_at = lax.axis_index("col")
    tensor_count = lax.axis_size("tensor")
    row_count = lax.axis_size("row")
    col_count = lax.axis_size("col")
    owners = tensor_count * row_count
    held = integral_tiles.shape[0]
    tile_size = integral_tiles.shape[2]
    owner = tile_index[:, 0] // AB * row_count + tile_index[:, 1] // MB
    earlier = jnp.arange(held)[:, None] > jnp.arange(held)[None, :]
    same_owner = owner[:, None] == owner[None, :]
    rank = jnp.sum(jnp.logical_and(earlier, same_owner), axis=1)
    position = owner * CAP + rank
    slots = owners * CAP
    send_tiles = jnp.zeros((slots, PB, tile_size), jnp.bfloat16).at[position].set(integral_tiles)
    send_index = jnp.full((slots, 3), -1, jnp.int32).at[position].set(tile_index)
    recv_tiles, recv_index = (
        lax.all_to_all(
            send_tiles.reshape(owners, CAP, PB, tile_size),
            ("tensor", "row"),
            split_axis=0,
            concat_axis=0,
            tiled=True,
        ),
        lax.all_to_all(
            send_index.reshape(owners, CAP, 3),
            ("tensor", "row"),
            split_axis=0,
            concat_axis=0,
            tiled=True,
        ),
    )
    recv_tiles = recv_tiles.reshape(slots, PB * tile_size)
    recv_index = recv_index.reshape(slots, 3)
    combos = AB * MB * NBC
    valid = recv_index[:, 0] >= 0
    local_aux = recv_index[:, 0] - tensor_at * AB
    local_mu = recv_index[:, 1] - row_at * MB
    local_nu = recv_index[:, 2] - col_at * NBC
    segment = jnp.where(valid, (local_aux * MB + local_mu) * NBC + local_nu, combos)
    selector = (jnp.arange(combos)[:, None] == segment[None, :]).astype(jnp.bfloat16)
    dense = jnp.dot(selector, recv_tiles, preferred_element_type=jnp.float32).astype(jnp.bfloat16)
    dense = dense.reshape(AB, MB, NBC, PB, TB, TB)
    virt_rows = virtual_coeff.shape[0]
    per_device = NV // (row_count * col_count)
    permuted = (
        virtual_coeff.reshape(virt_rows, row_count, col_count, per_device)
        .transpose(0, 2, 1, 3)
        .reshape(NBC, TB, NV)
    )
    half_rows = AB * MB * PB * TB
    product = jnp.einsum("knv,ajkpun->vajpu", permuted, dense, preferred_element_type=jnp.float32)
    half = lax.psum_scatter(
        product.reshape(NV // col_count * lax.axis_size("col"), half_rows).astype(jnp.bfloat16),
        "col",
        scatter_dimension=0,
        tiled=True,
    )
    occ_local = occupied_coeff.reshape(MB, TB, NOCC)
    picked = half.reshape(per_device * lax.axis_size("row"), AB, MB, PB, TB)
    product = jnp.einsum("vajpu,juo->vapo", picked, occ_local, preferred_element_type=jnp.float32)
    return lax.psum_scatter(
        product.reshape(per_device * lax.axis_size("row"), AB * PB, NOCC).astype(jnp.bfloat16),
        "row",
        scatter_dimension=0,
        tiled=True,
    )


LANES = 128
KD = 8
UP = TB * TB // LANES
ROWS = PB * UP
PAY = KD * ROWS + 16
CUT = PAY // 32 * 16
T, R, C = 2, 4, 4
VB = NV // (R * C)
NU = NBC * TB
MESH = pl.DeviceIdType.MESH


def gather_kernel(pay, virt, occ, tiles, coeff, occ_all, own_sem, zs, xs, ys, ss, rx, rh, rs, cs, cr, css, csr, os_, or_, oss, osr):
    t = lax.axis_index("tensor")
    r = lax.axis_index("row")
    c = lax.axis_index("col")
    sib = 1 - t
    y = r // 2
    x = r % 2
    rx_ = y * 2 + (1 - x)
    ry_ = (1 - y) * 2 + x
    rd_ = (1 - y) * 2 + (1 - x)
    sibling = (sib, r, c)
    xdev = (t, rx_, c)
    ydev = (t, ry_, c)
    ddev = (t, rd_, c)

    barrier = pltpu.get_barrier_semaphore()
    for dev in (sibling, xdev, ydev, ddev):
        pl.semaphore_signal(barrier, inc=1, device_id=dev, device_id_type=MESH)
    for d in range(1, C):
        pl.semaphore_signal(barrier, inc=1, device_id=(t, r, lax.rem(c + d, C)), device_id_type=MESH)
    pl.semaphore_wait(barrier, 7)

    def remote(src, dst, send, recv, dev):
        return pltpu.make_async_remote_copy(
            src_ref=src, dst_ref=dst, send_sem=send, recv_sem=recv, device_id=dev, device_id_type=MESH
        )

    def zcopy(z, way, dev, src=None):
        slot = tiles.at[z, r, t]
        return remote(slot if src is None else src, slot, zs.at[way, z], rx.at[z, r], dev)

    def xcopy(z, src=None):
        slot = tiles.at[z, r, t]
        return remote(slot if src is None else src, slot, xs.at[z], rx.at[z, r], xdev)

    def ycopy(z, src=None):
        slot = tiles.at[z, r, t]
        return remote(slot if src is None else src, slot, ys.at[z], rx.at[z, r], ydev)

    def scopy(z, row, src=None):
        slot = tiles.at[z, row, t]
        return remote(slot if src is None else src, slot, ss.at[z, row], rs.at[z, row], sibling)

    LOW, HIGH = pl.ds(0, CUT), pl.ds(CUT, PAY - CUT)

    def yhalf(z):
        slot = tiles.at[z, rx_, t, LOW]
        return remote(slot, slot, ys.at[C + z], rh.at[0, z], ydev)

    def xhalf(z):
        slot = tiles.at[z, ry_, t, HIGH]
        return remote(slot, slot, xs.at[C + z], rh.at[1, z], xdev)

    def shalf(part, z):
        slot = tiles.at[z, rd_, t, (LOW, HIGH)[part]]
        return remote(slot, slot, ss.at[C + part, z], rs.at[C + part, z], sibling)

    def wait_block(z, row, sem):
        slot = tiles.at[z, row, t]
        remote(slot, slot, zs.at[0, 0], sem, sibling).wait_recv()

    def wait_half(part, z):
        slot = tiles.at[z, rd_, t, (LOW, HIGH)[part]]
        remote(slot, slot, zs.at[0, 0], rh.at[part, z], sibling).wait_recv()

    half_nu = NU // T

    def ccopy(dest):
        return remote(
            virt.at[pl.ds(t * half_nu, half_nu), pl.ds(pl.multiple_of((r * C + dest) * VB, VB), VB)],
            coeff.at[c, t],
            cs.at[dest],
            cr.at[c],
            (t, r, dest),
        )

    def csib(z):
        slot = coeff.at[z, t]
        return remote(slot, slot, css.at[z], csr.at[z], sibling)

    occ_rows = occ.shape[1]

    def ocopy(row, dev, at):
        return remote(occ.at[t], occ_all.at[t, pl.ds(r * occ_rows, occ_rows)], os_.at[at], or_.at[r], dev)

    def osib(row):
        slot = occ_all.at[t, pl.ds(row * occ_rows, occ_rows)]
        return remote(slot, slot, oss.at[row], osr.at[row], sibling)

    @pl.when(c + 1 < C)
    def _():
        zcopy(c, 0, (t, r, c + 1), pay).start()

    @pl.when(c > 0)
    def _():
        zcopy(c, 1, (t, r, c - 1), pay).start()

    xcopy(c, pay).start()
    ycopy(c, pay).start()
    scopy(c, r, pay).start()
    own = pltpu.make_async_copy(pay, tiles.at[c, r, t], own_sem.at[0])
    own.start()
    own_c = pltpu.make_async_copy(
        virt.at[pl.ds(t * half_nu, half_nu), pl.ds(pl.multiple_of((r * C + c) * VB, VB), VB)],
        coeff.at[c, t],
        own_sem.at[1],
    )
    own_c.start()
    own_o = pltpu.make_async_copy(occ.at[t], occ_all.at[t, pl.ds(r * occ_rows, occ_rows)], own_sem.at[2])
    own_o.start()
    own_c.wait()
    csib(c).start()
    own_o.wait()
    osib(r).start()

    def line_block(z):
        xcopy(z).start()
        ycopy(z).start()
        scopy(z, r).start()

    def plane_blocks(z):
        wait_block(z, rx_, rx.at[z, rx_])
        yhalf(z).start()
        scopy(z, rx_).start()
        wait_block(z, ry_, rx.at[z, ry_])
        xhalf(z).start()
        scopy(z, ry_).start()

    def plane_halves(z):
        for part in range(2):
            wait_half(part, z)
            shalf(part, z).start()

    for d in range(1, C):
        @pl.when(c >= d)
        def _():
            wait_block(c - d, r, rx.at[c - d, r])

            @pl.when(c + 1 < C)
            def _():
                zcopy(c - d, 0, (t, r, c + 1)).start()

            line_block(c - d)

        @pl.when(c + d < C)
        def _():
            wait_block(c + d, r, rx.at[c + d, r])

            @pl.when(c > 0)
            def _():
                zcopy(c + d, 1, (t, r, c - 1)).start()

            line_block(c + d)

        if d == 1:
            for e in range(1, C):
                ccopy(lax.rem(c + e, C)).start()
            for at, (row, dev) in enumerate(((rx_, xdev), (ry_, ydev), (rd_, ddev))):
                ocopy(row, dev, at).start()
            plane_blocks(c)
        else:
            before = d - 1

            @pl.when(c >= before)
            def _():
                plane_blocks(c - before)

            @pl.when(c + before < C)
            def _():
                plane_blocks(c + before)

    for e in range(1, C):
        z = lax.rem(c + e, C)
        remote(coeff.at[z, t], coeff.at[z, t], zs.at[0, 0], cr.at[z], sibling).wait_recv()
        csib(z).start()
    for row in (rx_, ry_, rd_):
        slot = occ_all.at[t, pl.ds(row * occ_rows, occ_rows)]
        remote(slot, slot, zs.at[0, 0], or_.at[row], sibling).wait_recv()
        osib(row).start()

    @pl.when(c >= C - 1)
    def _():
        plane_blocks(c - (C - 1))

    @pl.when(c + C - 1 < C)
    def _():
        plane_blocks(c + (C - 1))

    plane_halves(c)
    for d in range(1, C):
        @pl.when(c >= d)
        def _():
            plane_halves(c - d)

        @pl.when(c + d < C)
        def _():
            plane_halves(c + d)

    own.wait()
    for z in range(C):
        for row in (r, rx_, ry_):
            slot = tiles.at[z, row, sib]
            remote(slot, slot, ss.at[z, row], rs.at[z, row], sibling).wait()
        slot = tiles.at[z, rd_, sib, LOW]
        remote(slot, slot, ss.at[C, z], rs.at[C, z], sibling).wait()
        slot = tiles.at[z, rd_, sib, HIGH]
        remote(slot, slot, ss.at[C + 1, z], rs.at[C + 1, z], sibling).wait()
        xcopy(z).wait_send()
        ycopy(z).wait_send()
        yhalf(z).wait_send()
        xhalf(z).wait_send()

        @pl.when(jnp.logical_and(z <= c, c + 1 < C))
        def _():
            zcopy(z, 0, sibling).wait_send()

        @pl.when(jnp.logical_and(z >= c, c > 0))
        def _():
            zcopy(z, 1, sibling).wait_send()

        slot = coeff.at[z, sib]
        remote(slot, slot, css.at[z], csr.at[z], sibling).wait()
    for e in range(1, C):
        ccopy(lax.rem(c + e, C)).wait_send()
    for at, (row, dev) in enumerate(((rx_, xdev), (ry_, ydev), (rd_, ddev))):
        ocopy(row, dev, at).wait_send()
    for row in range(R):
        slot = occ_all.at[sib, pl.ds(row * occ_rows, occ_rows)]
        remote(slot, slot, oss.at[row], osr.at[row], sibling).wait()


def transform_kernel(dest, block, tiles, coeff, occ, out, diag, acc, wide):
    step = pl.program_id(0)
    per_step = tiles.shape[0]

    @pl.when(step == 0)
    def _():
        acc[...] = jnp.zeros_like(acc)
        diag[...] = jnp.zeros_like(diag)

        def fill(n, _):
            piece = coeff[n]
            diag[n, 0:TB, 0:VB] = piece
            diag[n, TB : 2 * TB, VB : 2 * VB] = piece
            return 0

        lax.fori_loop(0, diag.shape[0], fill, 0)

    for j in range(per_step):
        for k in range(KD):
            at = (step * per_step + j) * KD + k
            to = dest[at]

            @pl.when(to >= 0)
            def _():
                part = jnp.dot(
                    tiles[j, k * ROWS : (k + 1) * ROWS, :], diag[block[at]], preferred_element_type=jnp.float32
                )
                acc[0, to] += part[:, 0:VB]
                acc[1, to] += part[:, VB : 2 * VB]

    @pl.when(step == pl.num_programs(0) - 1)
    def _():
        mus = R * MB
        for a in range(AB):
            def one(p, _):
                total = jnp.zeros((VB, NOCC), jnp.float32)
                for low in range(2):
                    rows = jnp.concatenate(
                        [
                            acc[low, a * mus + m, pl.ds(p, UP, stride=PB), :]
                            for m in range(mus)
                        ],
                        axis=0,
                    ).astype(jnp.bfloat16)
                    total += lax.dot_general(
                        rows, occ[low], (((0,), (0,)), ((), ())), preferred_element_type=jnp.float32
                    )
                for q in range(NOCC // LANES):
                    wide[q, pl.ds(a * PB + p, VB, stride=AB * PB), :] = total[:, q * LANES : (q + 1) * LANES]
                return 0

            lax.fori_loop(0, PB, one, 0)

        def put(i, _):
            v = pl.multiple_of(i * 8, 8)
            rows = pl.ds(pl.multiple_of(i * 8 * AB * PB, 8 * AB * PB), 8 * AB * PB)
            for q in range(NOCC // LANES):
                part = wide[q, rows, :].reshape(8, AB * PB, LANES).astype(jnp.bfloat16)
                out[pl.ds(v, 8), :, q * LANES : (q + 1) * LANES] = part
            return 0

        lax.fori_loop(0, VB // 8, put, 0)


def gathered(integral_tiles, tile_index, virtual_coeff, occupied_coeff):
    t = lax.axis_index("tensor")
    body = integral_tiles.reshape(KD, PB, UP, LANES).transpose(0, 2, 1, 3).reshape(KD * ROWS, LANES)
    index = jnp.pad(tile_index.astype(jnp.bfloat16), ((0, 16 - KD), (0, LANES - 3)))
    pay = jnp.concatenate([body, index], axis=0)
    occ = occupied_coeff.reshape(MB * TB // 2, 2, NOCC).transpose(1, 0, 2)
    dma = pltpu.SemaphoreType.DMA
    tiles, coeff, occ_all = pl.pallas_call(
        gather_kernel,
        out_shape=(
            jax.ShapeDtypeStruct((C, R, T, PAY, LANES), jnp.bfloat16),
            jax.ShapeDtypeStruct((C, T, NU // T, VB), jnp.bfloat16),
            jax.ShapeDtypeStruct((2, R * MB * TB // 2, NOCC), jnp.bfloat16),
        ),
        in_specs=[pl.BlockSpec(memory_space=pl.ANY)] * 3,
        out_specs=[pl.BlockSpec(memory_space=pl.ANY)] * 3,
        scratch_shapes=[
            dma((3,)),
            dma((2, C)),
            dma((2 * C,)),
            dma((2 * C,)),
            dma((C + 2, R)),
            dma((C, R)),
            dma((2, C)),
            dma((C + 2, R)),
            dma((C,)),
            dma((C,)),
            dma((C,)),
            dma((C,)),
            dma((3,)),
            dma((R,)),
            dma((R,)),
            dma((R,)),
        ],
        compiler_params=pltpu.CompilerParams(collective_id=0, has_side_effects=True),
        name="gather_tiles",
    )(pay, virtual_coeff, occ)
    sources = C * R * T
    flat = tiles.reshape(sources, PAY, LANES)
    found = flat[:, KD * ROWS : KD * ROWS + KD, 0:3].astype(jnp.int32).reshape(sources * KD, 3)
    aux = found[:, 0] - t * AB
    mine = jnp.logical_and(aux >= 0, aux < AB)
    dest = jnp.where(mine, aux * (R * MB) + found[:, 1], -1)
    per_step = 2
    return pl.pallas_call(
        transform_kernel,
        grid_spec=pltpu.PrefetchScalarGridSpec(
            num_scalar_prefetch=2,
            grid=(sources // per_step,),
            in_specs=[
                pl.BlockSpec((per_step, PAY, LANES), lambda s, *_: (s, 0, 0)),
                pl.BlockSpec((C * NBC, TB, VB), lambda s, *_: (0, 0, 0)),
                pl.BlockSpec((2, R * MB * TB // 2, NOCC), lambda s, *_: (0, 0, 0)),
            ],
            out_specs=pl.BlockSpec((VB, AB * PB, NOCC), lambda s, *_: (0, 0, 0)),
            scratch_shapes=[
                pltpu.VMEM((C * NBC, 2 * TB, 2 * VB), jnp.bfloat16),
                pltpu.VMEM((2, AB * R * MB, ROWS, VB), jnp.float32),
                pltpu.VMEM((NOCC // LANES, VB * AB * PB, LANES), jnp.float32),
            ],
        ),
        out_shape=jax.ShapeDtypeStruct((VB, AB * PB, NOCC), jnp.bfloat16),
        compiler_params=pltpu.CompilerParams(vmem_limit_bytes=40 * 1024 * 1024),
        name="transform_tiles",
    )(dest, found[:, 2], flat, coeff.reshape(C * NBC, TB, VB), occ_all)


def solution(mesh):
    in_specs = (
        P(("tensor", "row", "col"), None, None),
        P(("tensor", "row", "col"), None),
        P("col", None),
        P("row", None),
    )
    out_specs = P(("row", "col"), "tensor", None)
    sizes = tuple(mesh.shape[name] for name in ("tensor", "row", "col"))
    body = gathered if sizes == (2, 4, 4) else shards
    return jax.shard_map(body, mesh=mesh, in_specs=in_specs, out_specs=out_specs, check_vma=False)
```

```python
import jax
import jax.numpy as jnp
from jax import lax
from jax.experimental import pallas as pl
from jax.experimental.pallas import tpu as pltpu
from jax.sharding import PartitionSpec as P

TB = 64
PB = 8
AB = 2
MB = 2
NBC = 16
CAP = 2
NV = 2048
NOCC = 512


def shards(integral_tiles, tile_index, virtual_coeff, occupied_coeff):
    tensor_at = lax.axis_index("tensor")
    row_at = lax.axis_index("row")
    col_at = lax.axis_index("col")
    tensor_count = lax.axis_size("tensor")
    row_count = lax.axis_size("row")
    col_count = lax.axis_size("col")
    owners = tensor_count * row_count
    held = integral_tiles.shape[0]
    tile_size = integral_tiles.shape[2]
    owner = tile_index[:, 0] // AB * row_count + tile_index[:, 1] // MB
    earlier = jnp.arange(held)[:, None] > jnp.arange(held)[None, :]
    same_owner = owner[:, None] == owner[None, :]
    rank = jnp.sum(jnp.logical_and(earlier, same_owner), axis=1)
    position = owner * CAP + rank
    slots = owners * CAP
    send_tiles = jnp.zeros((slots, PB, tile_size), jnp.bfloat16).at[position].set(integral_tiles)
    send_index = jnp.full((slots, 3), -1, jnp.int32).at[position].set(tile_index)
    recv_tiles, recv_index = (
        lax.all_to_all(
            send_tiles.reshape(owners, CAP, PB, tile_size),
            ("tensor", "row"),
            split_axis=0,
            concat_axis=0,
            tiled=True,
        ),
        lax.all_to_all(
            send_index.reshape(owners, CAP, 3),
            ("tensor", "row"),
            split_axis=0,
            concat_axis=0,
            tiled=True,
        ),
    )
    recv_tiles = recv_tiles.reshape(slots, PB * tile_size)
    recv_index = recv_index.reshape(slots, 3)
    combos = AB * MB * NBC
    valid = recv_index[:, 0] >= 0
    local_aux = recv_index[:, 0] - tensor_at * AB
    local_mu = recv_index[:, 1] - row_at * MB
    local_nu = recv_index[:, 2] - col_at * NBC
    segment = jnp.where(valid, (local_aux * MB + local_mu) * NBC + local_nu, combos)
    selector = (jnp.arange(combos)[:, None] == segment[None, :]).astype(jnp.bfloat16)
    dense = jnp.dot(selector, recv_tiles, preferred_element_type=jnp.float32).astype(jnp.bfloat16)
    dense = dense.reshape(AB, MB, NBC, PB, TB, TB)
    virt_rows = virtual_coeff.shape[0]
    per_device = NV // (row_count * col_count)
    permuted = (
        virtual_coeff.reshape(virt_rows, row_count, col_count, per_device)
        .transpose(0, 2, 1, 3)
        .reshape(NBC, TB, NV)
    )
    half_rows = AB * MB * PB * TB
    product = jnp.einsum("knv,ajkpun->vajpu", permuted, dense, preferred_element_type=jnp.float32)
    half = lax.psum_scatter(
        product.reshape(NV // col_count * lax.axis_size("col"), half_rows).astype(jnp.bfloat16),
        "col",
        scatter_dimension=0,
        tiled=True,
    )
    occ_local = occupied_coeff.reshape(MB, TB, NOCC)
    picked = half.reshape(per_device * lax.axis_size("row"), AB, MB, PB, TB)
    product = jnp.einsum("vajpu,juo->vapo", picked, occ_local, preferred_element_type=jnp.float32)
    return lax.psum_scatter(
        product.reshape(per_device * lax.axis_size("row"), AB * PB, NOCC).astype(jnp.bfloat16),
        "row",
        scatter_dimension=0,
        tiled=True,
    )


LANES = 128
KD = 8
UP = TB * TB // LANES
ROWS = PB * UP
PAY = KD * ROWS + 16
G = 4
PIECE = KD * ROWS // G
LAST = PIECE + 16
T, R, C = 2, 4, 4
VB = NV // (R * C)
NU = NBC * TB
TILES_ALL = T * R * C * KD
MESH = pl.DeviceIdType.MESH


def gather_kernel(body, tail, virt, occ, tiles, coeff, occ_all, own_sem, zs, xs, ys, ss, rx, rs, cs, cr, css, csr, os_, or_, oss, osr):
    t = lax.axis_index("tensor")
    r = lax.axis_index("row")
    c = lax.axis_index("col")
    sib = 1 - t
    y = r // 2
    x = r % 2
    rx_ = y * 2 + (1 - x)
    ry_ = (1 - y) * 2 + x
    rd_ = (1 - y) * 2 + (1 - x)
    sibling = (sib, r, c)
    xdev = (t, rx_, c)
    ydev = (t, ry_, c)
    ddev = (t, rd_, c)
    up = (t, r, lax.rem(c + 1, C))
    down = (t, r, lax.rem(c + C - 1, C))

    barrier = pltpu.get_barrier_semaphore()
    for dev in (sibling, xdev, ydev, ddev):
        pl.semaphore_signal(barrier, inc=1, device_id=dev, device_id_type=MESH)
    for d in range(1, C):
        pl.semaphore_signal(barrier, inc=1, device_id=(t, r, lax.rem(c + d, C)), device_id_type=MESH)
    pl.semaphore_wait(barrier, 7)

    def remote(src, dst, send, recv, dev):
        return pltpu.make_async_remote_copy(
            src_ref=src, dst_ref=dst, send_sem=send, recv_sem=recv, device_id=dev, device_id_type=MESH
        )

    def spot(z, row, g, core=t):
        return tiles.at[z, row, core, pl.ds(g * PIECE, LAST if g == G - 1 else PIECE)]

    def mine(g):
        return tail if g == G - 1 else body.at[pl.ds(g * PIECE, PIECE)]

    def send(z, row, g, sem, dev, src=None):
        here = spot(z, row, g)
        return remote(here if src is None else src, here, sem, rx.at[z, row, g], dev)

    def share(z, row, g, src=None):
        here = spot(z, row, g)
        return remote(here if src is None else src, here, ss.at[z, row, g], rs.at[z, row, g], sibling)

    def arrived(z, row, g):
        here = spot(z, row, g)
        remote(here, here, zs.at[0, 0, 0], rx.at[z, row, g], sibling).wait_recv()

    half_nu = NU // T

    def own_virt(dest):
        return virt.at[pl.ds(t * half_nu, half_nu), pl.ds(pl.multiple_of((r * C + dest) * VB, VB), VB)]

    def ccopy(dest):
        return remote(own_virt(dest), coeff.at[c, t], cs.at[dest], cr.at[c], (t, r, dest))

    def csib(z):
        slot = coeff.at[z, t]
        return remote(slot, slot, css.at[z], csr.at[z], sibling)

    occ_rows = occ.shape[0] // T

    def occ_spot(row, core):
        return occ_all.at[pl.ds((row * T + core) * occ_rows, occ_rows)]

    own_occ = occ.at[pl.ds(t * occ_rows, occ_rows)]

    def ocopy(dev, at):
        return remote(own_occ, occ_spot(r, t), os_.at[at], or_.at[r], dev)

    def osib(row):
        return remote(occ_spot(row, t), occ_spot(row, t), oss.at[row], osr.at[row], sibling)

    def at_distance(d, act):
        if d == 0:
            act(c)
        else:
            pl.when(c >= d)(lambda: act(c - d))
            pl.when(c + d < C)(lambda: act(c + d))

    for g in range(G):
        pl.when(c + 1 < C)(lambda: send(c, r, g, zs.at[0, c, g], up, mine(g)).start())
        pl.when(c > 0)(lambda: send(c, r, g, zs.at[1, c, g], down, mine(g)).start())
        send(c, r, g, xs.at[0, c, g], xdev, mine(g)).start()
        send(c, r, g, ys.at[0, c, g], ydev, mine(g)).start()
    owns = [pltpu.make_async_copy(mine(g), spot(c, r, g), own_sem.at[g]) for g in range(G)]
    owns.append(pltpu.make_async_copy(own_virt(c), coeff.at[c, t], own_sem.at[G]))
    owns.append(pltpu.make_async_copy(own_occ, occ_spot(r, t), own_sem.at[G + 1]))
    for copy in owns:
        copy.start()
    for g in range(G):
        share(c, r, g, mine(g)).start()
    for at, dev in enumerate((xdev, ydev, ddev)):
        ocopy(dev, at).start()
    owns[G].wait()
    csib(c).start()
    owns[G + 1].wait()
    osib(r).start()

    def line(z, below):
        for g in range(G):
            arrived(z, r, g)
            if below:
                pl.when(c + 1 < C)(lambda: send(z, r, g, zs.at[0, z, g], up).start())
            else:
                pl.when(c > 0)(lambda: send(z, r, g, zs.at[1, z, g], down).start())
            send(z, r, g, xs.at[0, z, g], xdev).start()
            send(z, r, g, ys.at[0, z, g], ydev).start()
            share(z, r, g).start()

    def plane(z):
        for g in range(G):
            arrived(z, rx_, g)
            if g % 2 == 0:
                send(z, rx_, g, ys.at[1, z, g], ydev).start()
            share(z, rx_, g).start()
            arrived(z, ry_, g)
            if g % 2 == 1:
                send(z, ry_, g, xs.at[1, z, g], xdev).start()
            share(z, ry_, g).start()

    def corner(z):
        for g in range(G):
            arrived(z, rd_, g)
            share(z, rd_, g).start()

    for stage in range(1, C + 2):
        if stage < C:
            d = stage
            pl.when(c >= d)(lambda: line(c - d, True))
            pl.when(c + d < C)(lambda: line(c + d, False))
        if stage == C - 1:
            for e in range(1, C):
                ccopy(lax.rem(c + e, C)).start()
        if stage <= C:
            at_distance(stage - 1, plane)
        if stage >= 2:
            at_distance(stage - 2, corner)

    for e in range(1, C):
        z = lax.rem(c + e, C)
        remote(coeff.at[z, t], coeff.at[z, t], zs.at[0, 0, 0], cr.at[z], sibling).wait_recv()
        csib(z).start()
    for row in (rx_, ry_, rd_):
        remote(occ_spot(row, t), occ_spot(row, t), zs.at[0, 0, 0], or_.at[row], sibling).wait_recv()
        osib(row).start()

    for g in range(G):
        owns[g].wait()
        for z in range(C):
            for row in range(R):
                here = spot(z, row, g, sib)
                remote(here, here, ss.at[z, row, g], rs.at[z, row, g], sibling).wait()
            send(z, r, g, xs.at[0, z, g], xdev).wait_send()
            send(z, r, g, ys.at[0, z, g], ydev).wait_send()
            if g % 2 == 0:
                send(z, rx_, g, ys.at[1, z, g], ydev).wait_send()
            else:
                send(z, ry_, g, xs.at[1, z, g], xdev).wait_send()
            pl.when(jnp.logical_and(z <= c, c + 1 < C))(lambda: send(z, r, g, zs.at[0, z, g], sibling).wait_send())
            pl.when(jnp.logical_and(z >= c, c > 0))(lambda: send(z, r, g, zs.at[1, z, g], sibling).wait_send())
    for z in range(C):
        slot = coeff.at[z, sib]
        remote(slot, slot, css.at[z], csr.at[z], sibling).wait()
    for e in range(1, C):
        ccopy(lax.rem(c + e, C)).wait_send()
    for at, dev in enumerate((xdev, ydev, ddev)):
        ocopy(dev, at).wait_send()
    for row in range(R):
        remote(occ_spot(row, sib), occ_spot(row, sib), oss.at[row], osr.at[row], sibling).wait()


GROUPS = AB * R * MB
BLOCKS = C * NBC
AHEAD = 32
TOGETHER = 4


def transform_kernel(order, count, tiles, coeff, occ, out, diag, acc, wide, ring, occ_low, sems):
    rounds = (count[0] + TOGETHER - 1) // TOGETHER

    def fetch(s):
        tile = lax.rem(order[s], TILES_ALL)
        at = lax.rem(s, AHEAD)
        start = pl.multiple_of(lax.rem(tile, KD) * ROWS, ROWS)
        return pltpu.make_async_copy(tiles.at[tile // KD, pl.ds(start, ROWS)], ring.at[at], sems.at[at])

    lax.fori_loop(0, jnp.minimum(rounds * TOGETHER, AHEAD), lambda s, _: (fetch(s).start(), 0)[1], 0)
    zero_block = jnp.zeros((TB, VB), jnp.bfloat16)

    def fill(n, _):
        piece = coeff[n]
        diag[n, 0:TB, 0:VB] = piece
        diag[n, TB : 2 * TB, VB : 2 * VB] = piece
        diag[n, 0:TB, VB : 2 * VB] = zero_block
        diag[n, TB : 2 * TB, 0:VB] = zero_block
        return 0

    lax.fori_loop(0, BLOCKS, fill, 0, unroll=2)
    diag[BLOCKS] = jnp.zeros((2 * TB, 2 * VB), jnp.bfloat16)

    def clear(i, _):
        acc[:, i] = jnp.zeros((2, ROWS, VB), jnp.float32)
        return 0

    lax.fori_loop(0, GROUPS + 1, clear, 0)
    mus = R * MB
    for q in range(NOCC // LANES):
        wide[q, 0 : mus * TB, :] = occ[:, q * LANES : (q + 1) * LANES].astype(jnp.float32)
    for q in range(NOCC // LANES):
        for low in range(2):
            picked = wide[q, pl.ds(low, mus * TB // 2, stride=2), :]
            occ_low[low, :, q * LANES : (q + 1) * LANES] = picked.astype(jnp.bfloat16)

    def add(to, part):
        acc[0, to] += part[:, 0:VB]
        acc[1, to] += part[:, VB : 2 * VB]

    def one_round(i, _):
        first = i * TOGETHER
        for k in range(TOGETHER):
            fetch(first + k).wait()
        parts = []
        for k in range(0, TOGETHER, 2):
            code_a, code_b = order[first + k] // TILES_ALL, order[first + k + 1] // TILES_ALL
            to_a, to_b = code_a // BLOCKS, code_b // BLOCKS
            at = lax.rem(first + k, AHEAD)
            same = to_a == to_b
            weights = jnp.concatenate(
                [diag[lax.rem(code_a, BLOCKS)], diag[jnp.where(same, lax.rem(code_b, BLOCKS), BLOCKS)]], axis=0
            )
            both = jnp.concatenate([ring[at], ring[at + 1]], axis=1)
            parts.append((to_a, jnp.dot(both, weights, preferred_element_type=jnp.float32)))
        for to_a, part in parts:
            add(to_a, part)
        for k in range(0, TOGETHER, 2):
            code_a, code_b = order[first + k] // TILES_ALL, order[first + k + 1] // TILES_ALL
            at = lax.rem(first + k, AHEAD)

            @pl.when(code_a // BLOCKS != code_b // BLOCKS)
            def _():
                weights = diag[lax.rem(code_b, BLOCKS)]
                add(code_b // BLOCKS, jnp.dot(ring[at + 1], weights, preferred_element_type=jnp.float32))

        @pl.when(first + AHEAD < rounds * TOGETHER)
        def _():
            for k in range(TOGETHER):
                fetch(first + AHEAD + k).start()

        return 0

    lax.fori_loop(0, rounds, one_round, 0)

    for a in range(AB):
        def one(p, _):
            total = None
            for low in range(2):
                rows = jnp.concatenate(
                    [acc[low, a * mus + m, pl.ds(p, UP, stride=PB), :] for m in range(mus)], axis=0
                ).astype(jnp.bfloat16)
                part = lax.dot_general(
                    rows, occ_low[low], (((0,), (0,)), ((), ())), preferred_element_type=jnp.float32
                )
                total = part if total is None else total + part
            for q in range(NOCC // LANES):
                wide[q, pl.ds(a * PB + p, VB, stride=AB * PB), :] = total[:, q * LANES : (q + 1) * LANES]
            return 0

        lax.fori_loop(0, PB, one, 0, unroll=2)

    def put(i, _):
        v = pl.multiple_of(i * 8, 8)
        rows = pl.ds(pl.multiple_of(i * 8 * AB * PB, 8 * AB * PB), 8 * AB * PB)
        for q in range(NOCC // LANES):
            part = wide[q, rows, :].reshape(8, AB * PB, LANES).astype(jnp.bfloat16)
            out[pl.ds(v, 8), :, q * LANES : (q + 1) * LANES] = part
        return 0

    lax.fori_loop(0, VB // 8, put, 0)


def gathered(integral_tiles, tile_index, virtual_coeff, occupied_coeff):
    t = lax.axis_index("tensor")
    body = integral_tiles.reshape(KD, PB, UP, LANES).transpose(0, 2, 1, 3).reshape(KD * ROWS, LANES)
    index = jnp.pad(tile_index.astype(jnp.bfloat16), ((0, 16 - KD), (0, LANES - 3)))
    tail = jnp.concatenate([body[(G - 1) * PIECE :], index], axis=0)
    dma = pltpu.SemaphoreType.DMA
    tiles, coeff, occ_all = pl.pallas_call(
        gather_kernel,
        out_shape=(
            jax.ShapeDtypeStruct((C, R, T, PAY, LANES), jnp.bfloat16),
            jax.ShapeDtypeStruct((C, T, NU // T, VB), jnp.bfloat16),
            jax.ShapeDtypeStruct((R * MB * TB, NOCC), jnp.bfloat16),
        ),
        in_specs=[pl.BlockSpec(memory_space=pl.ANY)] * 4,
        out_specs=[pl.BlockSpec(memory_space=pl.ANY)] * 3,
        scratch_shapes=[
            dma((G + 2,)),
            dma((2, C, G)),
            dma((2, C, G)),
            dma((2, C, G)),
            dma((C, R, G)),
            dma((C, R, G)),
            dma((C, R, G)),
            dma((C,)),
            dma((C,)),
            dma((C,)),
            dma((C,)),
            dma((3,)),
            dma((R,)),
            dma((R,)),
            dma((R,)),
        ],
        compiler_params=pltpu.CompilerParams(collective_id=0, has_side_effects=True),
        name="gather_tiles",
    )(body, tail, virtual_coeff, occupied_coeff)
    sources = C * R * T
    flat = tiles.reshape(sources, PAY, LANES)
    found = flat[:, KD * ROWS : KD * ROWS + KD, 0:3].astype(jnp.int32).reshape(sources * KD, 3)
    aux = found[:, 0] - t * AB
    mine = jnp.logical_and(aux >= 0, aux < AB)
    group = jnp.where(mine, aux * (R * MB) + found[:, 1], GROUPS)
    code = (group * BLOCKS + found[:, 2]) * TILES_ALL + jnp.arange(TILES_ALL, dtype=jnp.int32)
    place = jnp.sum((code[None, :] < code[:, None]).astype(jnp.int32), axis=1)
    slots = jnp.arange(TILES_ALL, dtype=jnp.int32)
    order = jnp.sum(jnp.where(place[:, None] == slots[None, :], code[:, None], 0), axis=0)
    count = jnp.sum(mine.astype(jnp.int32)).reshape(1)
    whole = pl.BlockSpec(memory_space=pltpu.VMEM)
    return pl.pallas_call(
        transform_kernel,
        in_specs=[pl.BlockSpec(memory_space=pltpu.SMEM)] * 2 + [pl.BlockSpec(memory_space=pl.ANY), whole, whole],
        out_specs=whole,
        scratch_shapes=[
            pltpu.VMEM((BLOCKS + 1, 2 * TB, 2 * VB), jnp.bfloat16),
            pltpu.VMEM((2, GROUPS + 1, ROWS, VB), jnp.float32),
            pltpu.VMEM((NOCC // LANES, VB * AB * PB, LANES), jnp.float32),
            pltpu.VMEM((AHEAD, ROWS, LANES), jnp.bfloat16),
            pltpu.VMEM((2, R * MB * TB // 2, NOCC), jnp.bfloat16),
            pltpu.SemaphoreType.DMA((AHEAD,)),
        ],
        out_shape=jax.ShapeDtypeStruct((VB, AB * PB, NOCC), jnp.bfloat16),
        compiler_params=pltpu.CompilerParams(vmem_limit_bytes=40 * 1024 * 1024),
        name="transform_tiles",
    )(order, count, flat, coeff.reshape(BLOCKS, TB, VB), occ_all)


def solution(mesh):
    in_specs = (
        P(("tensor", "row", "col"), None, None),
        P(("tensor", "row", "col"), None),
        P("col", None),
        P("row", None),
    )
    out_specs = P(("row", "col"), "tensor", None)
    sizes = tuple(mesh.shape[name] for name in ("tensor", "row", "col"))
    body = gathered if sizes == (2, 4, 4) else shards
    return jax.shard_map(body, mesh=mesh, in_specs=in_specs, out_specs=out_specs, check_vma=False)
```

```python
import jax
import jax.numpy as jnp
from jax import lax
from jax.experimental import pallas as pl
from jax.experimental.pallas import tpu as pltpu
from jax.sharding import PartitionSpec as P

TB = 64
PB = 8
AB = 2
MB = 2
NBC = 16
CAP = 2
NV = 2048
NOCC = 512


def shards(integral_tiles, tile_index, virtual_coeff, occupied_coeff):
    tensor_at = lax.axis_index("tensor")
    row_at = lax.axis_index("row")
    col_at = lax.axis_index("col")
    tensor_count = lax.axis_size("tensor")
    row_count = lax.axis_size("row")
    col_count = lax.axis_size("col")
    owners = tensor_count * row_count
    held = integral_tiles.shape[0]
    tile_size = integral_tiles.shape[2]
    owner = tile_index[:, 0] // AB * row_count + tile_index[:, 1] // MB
    earlier = jnp.arange(held)[:, None] > jnp.arange(held)[None, :]
    same_owner = owner[:, None] == owner[None, :]
    rank = jnp.sum(jnp.logical_and(earlier, same_owner), axis=1)
    position = owner * CAP + rank
    slots = owners * CAP
    send_tiles = jnp.zeros((slots, PB, tile_size), jnp.bfloat16).at[position].set(integral_tiles)
    send_index = jnp.full((slots, 3), -1, jnp.int32).at[position].set(tile_index)
    recv_tiles, recv_index = (
        lax.all_to_all(
            send_tiles.reshape(owners, CAP, PB, tile_size),
            ("tensor", "row"),
            split_axis=0,
            concat_axis=0,
            tiled=True,
        ),
        lax.all_to_all(
            send_index.reshape(owners, CAP, 3),
            ("tensor", "row"),
            split_axis=0,
            concat_axis=0,
            tiled=True,
        ),
    )
    recv_tiles = recv_tiles.reshape(slots, PB * tile_size)
    recv_index = recv_index.reshape(slots, 3)
    combos = AB * MB * NBC
    valid = recv_index[:, 0] >= 0
    local_aux = recv_index[:, 0] - tensor_at * AB
    local_mu = recv_index[:, 1] - row_at * MB
    local_nu = recv_index[:, 2] - col_at * NBC
    segment = jnp.where(valid, (local_aux * MB + local_mu) * NBC + local_nu, combos)
    selector = (jnp.arange(combos)[:, None] == segment[None, :]).astype(jnp.bfloat16)
    dense = jnp.dot(selector, recv_tiles, preferred_element_type=jnp.float32).astype(jnp.bfloat16)
    dense = dense.reshape(AB, MB, NBC, PB, TB, TB)
    virt_rows = virtual_coeff.shape[0]
    per_device = NV // (row_count * col_count)
    permuted = (
        virtual_coeff.reshape(virt_rows, row_count, col_count, per_device)
        .transpose(0, 2, 1, 3)
        .reshape(NBC, TB, NV)
    )
    half_rows = AB * MB * PB * TB
    product = jnp.einsum("knv,ajkpun->vajpu", permuted, dense, preferred_element_type=jnp.float32)
    half = lax.psum_scatter(
        product.reshape(NV // col_count * lax.axis_size("col"), half_rows).astype(jnp.bfloat16),
        "col",
        scatter_dimension=0,
        tiled=True,
    )
    occ_local = occupied_coeff.reshape(MB, TB, NOCC)
    picked = half.reshape(per_device * lax.axis_size("row"), AB, MB, PB, TB)
    product = jnp.einsum("vajpu,juo->vapo", picked, occ_local, preferred_element_type=jnp.float32)
    return lax.psum_scatter(
        product.reshape(per_device * lax.axis_size("row"), AB * PB, NOCC).astype(jnp.bfloat16),
        "row",
        scatter_dimension=0,
        tiled=True,
    )


LANES = 128
KD = 8
UP = TB * TB // LANES
ROWS = PB * UP
PAY = KD * ROWS + 16
G = 2
PIECE = KD * ROWS // G
LAST = PIECE + 16
T, R, C = 2, 4, 4
VB = NV // (R * C)
NU = NBC * TB
TILES_ALL = T * R * C * KD
MESH = pl.DeviceIdType.MESH


def gather_kernel(body, tail, virt, occ, tiles, coeff, occ_all, own_sem, zs, xs, ys, ss, rx, rs, cs, cr, css, csr, os_, or_, oss, osr):
    t = lax.axis_index("tensor")
    r = lax.axis_index("row")
    c = lax.axis_index("col")
    sib = 1 - t
    y = r // 2
    x = r % 2
    rx_ = y * 2 + (1 - x)
    ry_ = (1 - y) * 2 + x
    rd_ = (1 - y) * 2 + (1 - x)
    sibling = (sib, r, c)
    xdev = (t, rx_, c)
    ydev = (t, ry_, c)
    ddev = (t, rd_, c)
    up = (t, r, lax.rem(c + 1, C))
    down = (t, r, lax.rem(c + C - 1, C))

    barrier = pltpu.get_barrier_semaphore()
    for dev in (sibling, xdev, ydev, ddev):
        pl.semaphore_signal(barrier, inc=1, device_id=dev, device_id_type=MESH)
    for d in range(1, C):
        pl.semaphore_signal(barrier, inc=1, device_id=(t, r, lax.rem(c + d, C)), device_id_type=MESH)
    pl.semaphore_wait(barrier, 7)

    def remote(src, dst, send, recv, dev):
        return pltpu.make_async_remote_copy(
            src_ref=src, dst_ref=dst, send_sem=send, recv_sem=recv, device_id=dev, device_id_type=MESH
        )

    def spot(z, row, g, core=t):
        return tiles.at[z, row, core, pl.ds(g * PIECE, LAST if g == G - 1 else PIECE)]

    def mine(g):
        return tail if g == G - 1 else body.at[pl.ds(g * PIECE, PIECE)]

    def send(z, row, g, sem, dev, src=None):
        here = spot(z, row, g)
        return remote(here if src is None else src, here, sem, rx.at[z, row, g], dev)

    def share(z, row, g, src=None):
        here = spot(z, row, g)
        return remote(here if src is None else src, here, ss.at[z, row, g], rs.at[z, row, g], sibling)

    def arrived(z, row, g):
        here = spot(z, row, g)
        remote(here, here, zs.at[0, 0, 0], rx.at[z, row, g], sibling).wait_recv()

    half_nu = NU // T

    def own_virt(dest):
        return virt.at[pl.ds(t * half_nu, half_nu), pl.ds(pl.multiple_of((r * C + dest) * VB, VB), VB)]

    def ccopy(dest):
        return remote(own_virt(dest), coeff.at[c, t], cs.at[dest], cr.at[c], (t, r, dest))

    def csib(z):
        slot = coeff.at[z, t]
        return remote(slot, slot, css.at[z], csr.at[z], sibling)

    occ_rows = occ.shape[0] // T

    def occ_spot(row, core):
        return occ_all.at[pl.ds((row * T + core) * occ_rows, occ_rows)]

    own_occ = occ.at[pl.ds(t * occ_rows, occ_rows)]

    def ocopy(dev, at):
        return remote(own_occ, occ_spot(r, t), os_.at[at], or_.at[r], dev)

    def osib(row):
        return remote(occ_spot(row, t), occ_spot(row, t), oss.at[row], osr.at[row], sibling)

    def at_distance(d, act):
        if d == 0:
            act(c)
        else:
            pl.when(c >= d)(lambda: act(c - d))
            pl.when(c + d < C)(lambda: act(c + d))

    for g in range(G):
        pl.when(c + 1 < C)(lambda: send(c, r, g, zs.at[0, c, g], up, mine(g)).start())
        pl.when(c > 0)(lambda: send(c, r, g, zs.at[1, c, g], down, mine(g)).start())
        send(c, r, g, xs.at[0, c, g], xdev, mine(g)).start()
        send(c, r, g, ys.at[0, c, g], ydev, mine(g)).start()
    owns = [pltpu.make_async_copy(mine(g), spot(c, r, g), own_sem.at[g]) for g in range(G)]
    owns.append(pltpu.make_async_copy(own_virt(c), coeff.at[c, t], own_sem.at[G]))
    owns.append(pltpu.make_async_copy(own_occ, occ_spot(r, t), own_sem.at[G + 1]))
    for copy in owns:
        copy.start()
    for g in range(G):
        share(c, r, g, mine(g)).start()
    for at, dev in enumerate((xdev, ydev, ddev)):
        ocopy(dev, at).start()

    def line(z, below):
        for g in range(G):
            arrived(z, r, g)
            if below:
                pl.when(c + 1 < C)(lambda: send(z, r, g, zs.at[0, z, g], up).start())
            else:
                pl.when(c > 0)(lambda: send(z, r, g, zs.at[1, z, g], down).start())
            share(z, r, g).start()

    def spread(z):
        for g in range(G):
            send(z, r, g, xs.at[0, z, g], xdev).start()
            send(z, r, g, ys.at[0, z, g], ydev).start()

    def plane(z):
        for g in range(G):
            arrived(z, rx_, g)
            if g % 2 == 0:
                send(z, rx_, g, ys.at[1, z, g], ydev).start()
            share(z, rx_, g).start()
            arrived(z, ry_, g)
            if g % 2 == 1:
                send(z, ry_, g, xs.at[1, z, g], xdev).start()
            share(z, ry_, g).start()

    def corner(z):
        for g in range(G):
            arrived(z, rd_, g)
            share(z, rd_, g).start()

    for stage in range(1, C + 2):
        if stage < C:
            d = stage
            pl.when(c >= d)(lambda: line(c - d, True))
            pl.when(c + d < C)(lambda: line(c + d, False))
            at_distance(d, spread)
        if stage == C - 1:
            for e in range(1, C):
                ccopy(lax.rem(c + e, C)).start()
        if stage <= C:
            at_distance(stage - 1, plane)
        if stage >= 2:
            at_distance(stage - 2, corner)

    owns[G].wait()
    csib(c).start()
    owns[G + 1].wait()
    osib(r).start()
    for e in range(1, C):
        z = lax.rem(c + e, C)
        remote(coeff.at[z, t], coeff.at[z, t], zs.at[0, 0, 0], cr.at[z], sibling).wait_recv()
        csib(z).start()
    for row in (rx_, ry_, rd_):
        remote(occ_spot(row, t), occ_spot(row, t), zs.at[0, 0, 0], or_.at[row], sibling).wait_recv()
        osib(row).start()

    for g in range(G):
        owns[g].wait()
        for z in range(C):
            for row in range(R):
                here = spot(z, row, g, sib)
                remote(here, here, ss.at[z, row, g], rs.at[z, row, g], sibling).wait()
            send(z, r, g, xs.at[0, z, g], xdev).wait_send()
            send(z, r, g, ys.at[0, z, g], ydev).wait_send()
            if g % 2 == 0:
                send(z, rx_, g, ys.at[1, z, g], ydev).wait_send()
            else:
                send(z, ry_, g, xs.at[1, z, g], xdev).wait_send()
            pl.when(jnp.logical_and(z <= c, c + 1 < C))(lambda: send(z, r, g, zs.at[0, z, g], sibling).wait_send())
            pl.when(jnp.logical_and(z >= c, c > 0))(lambda: send(z, r, g, zs.at[1, z, g], sibling).wait_send())
    for z in range(C):
        slot = coeff.at[z, sib]
        remote(slot, slot, css.at[z], csr.at[z], sibling).wait()
    for e in range(1, C):
        ccopy(lax.rem(c + e, C)).wait_send()
    for at, dev in enumerate((xdev, ydev, ddev)):
        ocopy(dev, at).wait_send()
    for row in range(R):
        remote(occ_spot(row, sib), occ_spot(row, sib), oss.at[row], osr.at[row], sibling).wait()


GROUPS = AB * R * MB
BLOCKS = C * NBC
AHEAD = 32
TOGETHER = 16


def transform_kernel(order, count, tiles, coeff, occ, out, diag, acc, wide, ring, occ_low, sems):
    rounds = (count[0] + TOGETHER - 1) // TOGETHER

    def fetch(s):
        tile = lax.rem(order[s], TILES_ALL)
        at = lax.rem(s, AHEAD)
        start = pl.multiple_of(lax.rem(tile, KD) * ROWS, ROWS)
        return pltpu.make_async_copy(tiles.at[tile // KD, pl.ds(start, ROWS)], ring.at[at], sems.at[at])

    lax.fori_loop(0, jnp.minimum(rounds * TOGETHER, AHEAD), lambda s, _: (fetch(s).start(), 0)[1], 0)
    zero_block = jnp.zeros((TB, VB), jnp.bfloat16)

    def fill(n, _):
        piece = coeff[n]
        diag[n, 0:TB, 0:VB] = piece
        diag[n, TB : 2 * TB, VB : 2 * VB] = piece
        diag[n, 0:TB, VB : 2 * VB] = zero_block
        diag[n, TB : 2 * TB, 0:VB] = zero_block
        return 0

    lax.fori_loop(0, BLOCKS, fill, 0, unroll=2)
    diag[BLOCKS] = jnp.zeros((2 * TB, 2 * VB), jnp.bfloat16)

    def clear(i, _):
        acc[:, i] = jnp.zeros((2, ROWS, VB), jnp.float32)
        return 0

    lax.fori_loop(0, GROUPS + 1, clear, 0)
    mus = R * MB
    for q in range(NOCC // LANES):
        wide[q, 0 : mus * TB, :] = occ[:, q * LANES : (q + 1) * LANES].astype(jnp.float32)
    for q in range(NOCC // LANES):
        for low in range(2):
            picked = wide[q, pl.ds(low, mus * TB // 2, stride=2), :]
            occ_low[low, :, q * LANES : (q + 1) * LANES] = picked.astype(jnp.bfloat16)

    def add(to, part):
        acc[0, to] += part[:, 0:VB]
        acc[1, to] += part[:, VB : 2 * VB]

    def one_round(i, _):
        first = i * TOGETHER
        for k in range(TOGETHER):
            fetch(first + k).wait()
        parts = []
        for k in range(0, TOGETHER, 2):
            code_a, code_b = order[first + k] // TILES_ALL, order[first + k + 1] // TILES_ALL
            to_a, to_b = code_a // BLOCKS, code_b // BLOCKS
            at = lax.rem(first + k, AHEAD)
            same = to_a == to_b
            weights = jnp.concatenate(
                [diag[lax.rem(code_a, BLOCKS)], diag[jnp.where(same, lax.rem(code_b, BLOCKS), BLOCKS)]], axis=0
            )
            both = jnp.concatenate([ring[at], ring[at + 1]], axis=1)
            parts.append((to_a, jnp.dot(both, weights, preferred_element_type=jnp.float32)))
        for to_a, part in parts:
            add(to_a, part)
        for k in range(0, TOGETHER, 2):
            code_a, code_b = order[first + k] // TILES_ALL, order[first + k + 1] // TILES_ALL
            at = lax.rem(first + k, AHEAD)

            @pl.when(code_a // BLOCKS != code_b // BLOCKS)
            def _():
                weights = diag[lax.rem(code_b, BLOCKS)]
                add(code_b // BLOCKS, jnp.dot(ring[at + 1], weights, preferred_element_type=jnp.float32))

        @pl.when(first + AHEAD < rounds * TOGETHER)
        def _():
            for k in range(TOGETHER):
                fetch(first + AHEAD + k).start()

        return 0

    lax.fori_loop(0, rounds, one_round, 0)

    for a in range(AB):
        def one(p, _):
            total = None
            for low in range(2):
                rows = jnp.concatenate(
                    [acc[low, a * mus + m, pl.ds(p, UP, stride=PB), :] for m in range(mus)], axis=0
                ).astype(jnp.bfloat16)
                part = lax.dot_general(
                    rows, occ_low[low], (((0,), (0,)), ((), ())), preferred_element_type=jnp.float32
                )
                total = part if total is None else total + part
            for q in range(NOCC // LANES):
                wide[q, pl.ds(a * PB + p, VB, stride=AB * PB), :] = total[:, q * LANES : (q + 1) * LANES]
            return 0

        lax.fori_loop(0, PB, one, 0, unroll=2)

    def put(i, _):
        v = pl.multiple_of(i * 8, 8)
        rows = pl.ds(pl.multiple_of(i * 8 * AB * PB, 8 * AB * PB), 8 * AB * PB)
        for q in range(NOCC // LANES):
            part = wide[q, rows, :].reshape(8, AB * PB, LANES).astype(jnp.bfloat16)
            out[pl.ds(v, 8), :, q * LANES : (q + 1) * LANES] = part
        return 0

    lax.fori_loop(0, VB // 8, put, 0)


def gathered(integral_tiles, tile_index, virtual_coeff, occupied_coeff):
    t = lax.axis_index("tensor")
    body = integral_tiles.reshape(KD, PB, UP, LANES).transpose(0, 2, 1, 3).reshape(KD * ROWS, LANES)
    index = jnp.pad(tile_index.astype(jnp.bfloat16), ((0, 16 - KD), (0, LANES - 3)))
    tail = jnp.concatenate([body[(G - 1) * PIECE :], index], axis=0)
    dma = pltpu.SemaphoreType.DMA
    tiles, coeff, occ_all = pl.pallas_call(
        gather_kernel,
        out_shape=(
            jax.ShapeDtypeStruct((C, R, T, PAY, LANES), jnp.bfloat16),
            jax.ShapeDtypeStruct((C, T, NU // T, VB), jnp.bfloat16),
            jax.ShapeDtypeStruct((R * MB * TB, NOCC), jnp.bfloat16),
        ),
        in_specs=[pl.BlockSpec(memory_space=pl.ANY)] * 4,
        out_specs=[pl.BlockSpec(memory_space=pl.ANY)] * 3,
        scratch_shapes=[
            dma((G + 2,)),
            dma((2, C, G)),
            dma((2, C, G)),
            dma((2, C, G)),
            dma((C, R, G)),
            dma((C, R, G)),
            dma((C, R, G)),
            dma((C,)),
            dma((C,)),
            dma((C,)),
            dma((C,)),
            dma((3,)),
            dma((R,)),
            dma((R,)),
            dma((R,)),
        ],
        compiler_params=pltpu.CompilerParams(collective_id=0, has_side_effects=True),
        name="gather_tiles",
    )(body, tail, virtual_coeff, occupied_coeff)
    sources = C * R * T
    flat = tiles.reshape(sources, PAY, LANES)
    found = flat[:, KD * ROWS : KD * ROWS + KD, 0:3].astype(jnp.int32).reshape(sources * KD, 3)
    aux = found[:, 0] - t * AB
    mine = jnp.logical_and(aux >= 0, aux < AB)
    group = jnp.where(mine, aux * (R * MB) + found[:, 1], GROUPS)
    code = (group * BLOCKS + found[:, 2]) * TILES_ALL + jnp.arange(TILES_ALL, dtype=jnp.int32)
    place = jnp.sum((code[None, :] < code[:, None]).astype(jnp.int32), axis=1)
    slots = jnp.arange(TILES_ALL, dtype=jnp.int32)
    order = jnp.sum(jnp.where(place[:, None] == slots[None, :], code[:, None], 0), axis=0)
    count = jnp.sum(mine.astype(jnp.int32)).reshape(1)
    whole = pl.BlockSpec(memory_space=pltpu.VMEM)
    return pl.pallas_call(
        transform_kernel,
        in_specs=[pl.BlockSpec(memory_space=pltpu.SMEM)] * 2 + [pl.BlockSpec(memory_space=pl.ANY), whole, whole],
        out_specs=whole,
        scratch_shapes=[
            pltpu.VMEM((BLOCKS + 1, 2 * TB, 2 * VB), jnp.bfloat16),
            pltpu.VMEM((2, GROUPS + 1, ROWS, VB), jnp.float32),
            pltpu.VMEM((NOCC // LANES, VB * AB * PB, LANES), jnp.float32),
            pltpu.VMEM((AHEAD, ROWS, LANES), jnp.bfloat16),
            pltpu.VMEM((2, R * MB * TB // 2, NOCC), jnp.bfloat16),
            pltpu.SemaphoreType.DMA((AHEAD,)),
        ],
        out_shape=jax.ShapeDtypeStruct((VB, AB * PB, NOCC), jnp.bfloat16),
        compiler_params=pltpu.CompilerParams(vmem_limit_bytes=40 * 1024 * 1024),
        name="transform_tiles",
    )(order, count, flat, coeff.reshape(BLOCKS, TB, VB), occ_all)


def solution(mesh):
    in_specs = (
        P(("tensor", "row", "col"), None, None),
        P(("tensor", "row", "col"), None),
        P("col", None),
        P("row", None),
    )
    out_specs = P(("row", "col"), "tensor", None)
    sizes = tuple(mesh.shape[name] for name in ("tensor", "row", "col"))
    body = gathered if sizes == (2, 4, 4) else shards
    return jax.shard_map(body, mesh=mesh, in_specs=in_specs, out_specs=out_specs, check_vma=False)
```
